32 devices in a mesh: dp: 4 (over x, core), fsdp: 8 (over z, y).
Axes of the slice: x: 2, y: 2, z: 4, core: 2. Of those that a mesh axis runs over, the one named last changes fastest.
Arguments:
- query_in: bfloat16 [7168, 1024], P(('dp', 'fsdp')), may hold values from -32 to 32
- key_in: bfloat16 [7168, 1024], P(('dp', 'fsdp')), may hold values from -32 to 32
- value_in: bfloat16 [7168, 1024], P(('dp', 'fsdp')), may hold values from -6 to 6
- length_plan: int32 [32, 224], P(('dp', 'fsdp')), may hold values from 0 to 223, each once within a row
- segment_ids: int32 [32, 224], P(('dp', 'fsdp')), may hold values from 0 to 3, never falling along the last dimension, each value on 1 to 112 neighbouring positions
- out_grad: bfloat16 [7168, 1024], P(('dp', 'fsdp')), may hold values from -6 to 6
- query_gain: float32 [128], replicated, may hold values from 0.7 to 6
- key_gain: float32 [128], replicated, may hold values from 0.7 to 6
Outputs:
- query_grad: bfloat16 [7168, 1024], P(('dp', 'fsdp'))
- key_grad: bfloat16 [7168, 1024], P(('dp', 'fsdp'))
- value_grad: bfloat16 [7168, 1024], P(('dp', 'fsdp'))
- query_gain_grad: float32 [128], replicated
- key_gain_grad: float32 [128], replicated
The draws below stay inside these ranges and needn't reach their ends.
Inputs may be any that keep to these rules, and one draw needn't show every extreme that they name: `length_plan`: each row is a permutation of 0 to 223. `segment_ids`: within a row the numbers never fall; each utterance piece holds 1 to 112 frames, and one holds exactly 112.
All inputs are finite; a program needn't handle non-finite values.
Results may differ from the reference program's by a relative error of at most 0.01.
The reference program's roundings to bfloat16 on the way count: a program that leaves them out, or rounds other values in their place, can miss the bound.
Values may be sent and summed in bfloat16 or wider, within the bound.
A program may use at most 64 MiB of HBM per device.

```python
import math
import jax
import jax.numpy as jnp
import numpy as np
from jax import lax

HEADS = 8
HEAD = 128
TOK_DEV = 224
SEGMENTS = 4
HID = 1024
SEGMAX = 112
DEVROWS = 32
FRAMES = 7168
N_DP = 4
N_FSDP = 8


def query_key_fields(key):
    base_key = jax.random.fold_in(key, 101)
    subkeys = jax.random.split(base_key, 5)
    width = HEADS * HEAD
    col_scale = jnp.exp(jax.random.uniform(subkeys[0], (HEAD,), jnp.float32, jnp.log(0.4), jnp.log(4.0)))
    col_scale = jnp.tile(col_scale, HEADS)
    row_query = jnp.exp(jax.random.uniform(subkeys[1], (FRAMES, 1), jnp.float32, jnp.log(0.3), jnp.log(3.0)))
    row_key = jnp.exp(jax.random.uniform(subkeys[2], (FRAMES, 1), jnp.float32, jnp.log(0.3), jnp.log(3.0)))
    noise_query = jax.random.normal(subkeys[3], (FRAMES, width), jnp.float32)
    noise_key = jax.random.normal(subkeys[4], (FRAMES, width), jnp.float32)
    key_field = noise_key
    query_field = noise_query
    query_out = jnp.clip(query_field * col_scale * row_query, -32.0, 32.0)
    key_out = jnp.clip(key_field * col_scale * row_key, -32.0, 32.0)
    return (query_out, key_out)


def draw_query_in(key, part):
    return query_key_fields(key)[0].astype(jnp.bfloat16)


def draw_key_in(key, part):
    return query_key_fields(key)[1].astype(jnp.bfloat16)


def draw_gain(key, salt):
    gain_key = jax.random.fold_in(key, salt)
    return jax.random.uniform(gain_key, (HEAD,), jnp.float32, 0.7, 1.6)


def draw_query_gain(key, part):
    return draw_gain(key, 202)


def draw_key_gain(key, part):
    return draw_gain(key, 303)


def block_scale(stream_key, shape, shards, least, largest):
    loudness = 1.0
    for axis_at, parts in shards:
        heights = jax.random.uniform(jax.random.fold_in(jax.random.fold_in(stream_key, 6), axis_at), (parts,), jnp.float32, least / len(shards), largest / len(shards))
        loudness = loudness * jnp.repeat(jnp.exp(heights), shape[axis_at] // parts).reshape((-1,) + (1,) * (len(shape) - 1 - axis_at))
    return loudness


def split_up(amount, total, bound, skew):
    weights = [(1 << 20) // math.isqrt(rank ** skew) + 1 for rank in range(2, amount + 1)]
    surplus, holding = total - bound - (amount - 1), [1] * (amount - 1)
    while surplus > 0:
        free = [i for i in range(amount - 1) if holding[i] < bound]
        mass, remaining = sum([weights[i] for i in free]), surplus
        for i in free:
            more = min(bound - holding[i], max(1, remaining * weights[i] // mass), surplus)
            holding[i] = holding[i] + more
            surplus = surplus - more
    return np.array([bound] + holding)


def ragged_sizes(stream_key, amount, total, limit, slope):
    if amount == 2:
        one = jax.random.randint(stream_key, (), max(1, total - limit), min(limit, total - 1) + 1)
        return jnp.stack([one, total - one])
    tallies = jnp.asarray(split_up(amount, total, limit, slope), jnp.int32)
    pairs = (amount - 1) // 2
    giver, sink = tallies[1:1 + 2 * pairs:2], tallies[2:2 + 2 * pairs:2]
    room = jnp.minimum(giver - 1, limit - sink)
    shifted = jax.random.randint(jax.random.fold_in(stream_key, 1), (pairs,), 0, 1 << 20) % (room + 1)
    tallies = tallies.at[1:1 + 2 * pairs:2].set(giver - shifted).at[2:2 + 2 * pairs:2].set(sink + shifted)
    return tallies[jax.random.permutation(jax.random.fold_in(stream_key, 2), amount)]


def bell_draw(stream_key, shape, scale, limit, shards=(), kind=jnp.bfloat16):
    values = scale * jax.random.normal(stream_key, shape, jnp.float32)
    if shards:
        values = values * block_scale(stream_key, shape, shards, -0.22, 0.18)
    return jnp.clip(values, -limit, limit).astype(kind)


def setup_inputs(seed: int = 0) -> dict:
    seeds = jax.random.split(jax.random.key(seed), 9)
    return {
        "query_in": draw_query_in(jax.random.fold_in(seeds[8], 71), 0),
        "key_in": draw_key_in(jax.random.fold_in(seeds[8], 71), 0),
        "value_in": bell_draw(seeds[2], (FRAMES, HID), 1.0, 6.0, ((0, 32),)),
        "length_plan": jax.vmap(lambda own: jax.random.permutation(own, TOK_DEV))(jax.random.split(seeds[3], DEVROWS)).reshape((DEVROWS, TOK_DEV)).astype(jnp.int32),
        "segment_ids": jax.vmap(lambda own: jnp.searchsorted(jnp.cumsum(ragged_sizes(own, SEGMENTS, TOK_DEV, SEGMAX, 2)), jnp.arange(TOK_DEV), side="right"))(jax.random.split(seeds[4], DEVROWS)).reshape((DEVROWS, TOK_DEV)).astype(jnp.int32),
        "out_grad": bell_draw(seeds[5], (FRAMES, HID), 1.0, 6.0, ((0, 32),)),
        "query_gain": draw_query_gain(jax.random.fold_in(seeds[8], 71), 0),
        "key_gain": draw_key_gain(jax.random.fold_in(seeds[8], 71), 0),
    }


def normalize(raw, gain):
    frames = raw.shape[0]
    values = raw.astype(jnp.float32).reshape(frames, HEADS, HEAD)
    inv_rms = lax.rsqrt(lax.optimization_barrier(jnp.mean(values * values, axis=-1, keepdims=True)) + 1e-06)
    unit_vec = values * inv_rms
    rounded = lax.optimization_barrier((unit_vec * gain).astype(jnp.bfloat16))
    return (unit_vec, inv_rms, rounded.astype(jnp.float32))

def norm_back(d_norm, unit_vec, inv_rms, gain):
    d_unit = d_norm * gain
    inner = lax.optimization_barrier(jnp.mean(d_unit * unit_vec, axis=-1, keepdims=True))
    result = inv_rms * (d_unit - unit_vec * inner)
    return result.reshape(result.shape[0], -1).astype(jnp.bfloat16)

def attend(query_in, key_in, value_in, segment_row, out_grad, query_gain, key_gain):
    frames = query_in.shape[0]
    score_scale = HEAD ** (-0.5)
    q_unit, q_inv, q_wide = normalize(query_in, query_gain)
    k_unit, k_inv, k_wide = normalize(key_in, key_gain)
    values_in = value_in.reshape(frames, HEADS, HEAD).astype(jnp.float32)
    grad_heads = out_grad.reshape(frames, HEADS, HEAD).astype(jnp.float32)
    scores = jnp.einsum('thd,shd->hts', q_wide, k_wide) * score_scale
    same_seg = segment_row[:, None] == segment_row[None, :]
    scores = jnp.where(same_seg[None], scores, -jnp.inf)
    row_max = lax.optimization_barrier(jnp.max(scores, axis=-1, keepdims=True))
    exponent = jnp.exp(scores - row_max)
    attn_probs = exponent / lax.optimization_barrier(jnp.sum(exponent, axis=-1, keepdims=True))
    probs_wide = lax.optimization_barrier(attn_probs.astype(jnp.bfloat16)).astype(jnp.float32)
    output = jnp.einsum('hts,shd->thd', probs_wide, values_in)
    row_delta = lax.optimization_barrier(jnp.sum(grad_heads * output, axis=-1))
    value_grad = jnp.einsum('hts,thd->shd', probs_wide, grad_heads).astype(jnp.bfloat16).reshape(frames, -1)
    d_prob = jnp.einsum('thd,shd->hts', grad_heads, values_in)
    d_score = (attn_probs * (d_prob - row_delta.T[:, :, None]) * score_scale).astype(jnp.bfloat16)
    d_score = lax.optimization_barrier(d_score).astype(jnp.float32)
    d_qnorm = jnp.einsum('hts,shd->thd', d_score, k_wide)
    d_knorm = jnp.einsum('hts,thd->shd', d_score, q_wide)
    query_part = lax.optimization_barrier(jnp.sum(d_qnorm * q_unit, axis=(0, 1)))
    key_part = lax.optimization_barrier(jnp.sum(d_knorm * k_unit, axis=(0, 1)))
    query_grad = norm_back(d_qnorm, q_unit, q_inv, query_gain)
    key_grad = norm_back(d_knorm, k_unit, k_inv, key_gain)
    return (query_grad, key_grad, value_grad, query_part, key_part)

def reference(query_in, key_in, value_in, length_plan, segment_ids, out_grad, query_gain, key_gain):
    devices = N_DP * N_FSDP
    block_rows = TOK_DEV // N_DP
    width = query_in.shape[1]
    positions = jnp.arange(TOK_DEV, dtype=jnp.int32)
    inverse = jax.vmap(lambda plan_row: jnp.zeros((TOK_DEV,), jnp.int32).at[plan_row].set(positions))(length_plan)

    def repack(source):
        rows_in = source.reshape(devices, TOK_DEV, width)
        outgoing = jax.vmap(lambda table, index: table[index])(rows_in, inverse)
        outgoing = outgoing.reshape(N_DP, N_FSDP, N_DP, block_rows, width)
        return jnp.transpose(outgoing, (2, 1, 0, 3, 4)).reshape(devices, TOK_DEV, width)
    packed_query = repack(query_in)
    packed_key = repack(key_in)
    packed_value = repack(value_in)
    grad_rows = out_grad.reshape(devices, TOK_DEV, width)

    def attend_device(device_items):
        query_dev, key_dev, value_dev, segment_row, grad_dev = device_items
        return attend(query_dev, key_dev, value_dev, segment_row, grad_dev, query_gain, key_gain)
    query_grad, key_grad, value_grad, query_part, key_part = lax.map(attend_device, (packed_query, packed_key, packed_value, segment_ids, grad_rows))
    return (query_grad.reshape(FRAMES, width), key_grad.reshape(FRAMES, width), value_grad.reshape(FRAMES, width), lax.optimization_barrier(jnp.sum(query_part, axis=0)), lax.optimization_barrier(jnp.sum(key_part, axis=0)))
```

```python
import functools
import math

import jax
import jax.numpy as jnp
from jax import lax
from jax.experimental import pallas as pl
from jax.experimental.pallas import tpu as pltpu
from jax.sharding import PartitionSpec as P

HEAD = 128
PER = 2
MESH = pl.DeviceIdType.MESH
F32, BF16 = jnp.float32, jnp.bfloat16


def mm(a, b, contract):
    return lax.dot_general(a, b, ((contract[:1], contract[1:]), ((), ())), preferred_element_type=F32)


def kernel(
    n_dp, n_fs,
    q_hbm, k_hbm, v_hbm, plan_ref, seg_ref, g_hbm, qgain_ref, kgain_ref,
    qgrad_ref, kgrad_ref, vgrad_ref, qsum_ref, ksum_ref,
    q_in, k_in, v_in, g_in, send, recv, onehot, bias, acc, red_dp, red_fs,
    in_sem, send_sem, recv_sem, dp_send, dp_recv, fs_send, fs_recv,
):
    frames = q_in.shape[0]
    rows = frames // n_dp
    chunks, _, height, _ = send.shape
    padded = height // (3 * PER)
    width = PER * HEAD
    me = lax.axis_index("dp")
    mf = lax.axis_index("fsdp")

    loads = [
        pltpu.make_async_copy(src, dst, in_sem.at[i])
        for i, (src, dst) in enumerate(((q_hbm, q_in), (k_hbm, k_in), (v_hbm, v_in), (g_hbm, g_in)))
    ]
    for load in loads:
        load.start()
    barrier = pltpu.get_barrier_semaphore()
    for k in range(1, n_dp):
        pl.semaphore_signal(barrier, inc=1, device_id={"dp": lax.rem(me + k, n_dp)}, device_id_type=MESH)
    for k in range(1, n_fs):
        pl.semaphore_signal(barrier, inc=1, device_id={"fsdp": lax.rem(mf + k, n_fs)}, device_id_type=MESH)

    order = lax.broadcasted_iota(jnp.int32, (n_dp * padded, 1), 0)
    if padded != rows:
        within = order % padded
        order = jnp.where(within < rows, order // padded * rows + within, -1)
    onehot[...] = (order == plan_ref[...]).astype(F32).astype(BF16)
    for load in loads[:3]:
        load.wait()

    def hop(c, k):
        to = lax.rem(me + k, n_dp)
        return pltpu.make_async_remote_copy(
            src_ref=send.at[c, to], dst_ref=recv.at[c, me],
            send_sem=send_sem.at[c, k], recv_sem=recv_sem.at[c, k],
            device_id={"dp": to}, device_id_type=MESH,
        )

    def stay(c):
        return pltpu.make_async_copy(send.at[c, me], recv.at[c, me], recv_sem.at[c, 0])

    def gather(c):
        cols = pl.ds(pl.multiple_of(c * width, width), width)
        sorted_rows = [mm(onehot[...], ref[:, cols], (1, 0)) for ref in (q_in, k_in, v_in)]
        for d in range(n_dp):
            span = slice(d * padded, (d + 1) * padded)
            send[c, d] = jnp.concatenate(
                [x[span, i * HEAD:(i + 1) * HEAD] for i in range(PER) for x in sorted_rows], axis=0
            ).astype(BF16)

    def launch(c):
        for k in range(1, n_dp):
            hop(c, k).start()
        stay(c).start()

    gather(0)
    pl.semaphore_wait(barrier, n_dp - 1 + n_fs - 1)
    launch(0)

    @pl.loop(1, chunks)
    def _(c):
        gather(c)
        launch(c)

    seg_row = jnp.broadcast_to(seg_ref[...].astype(F32), (frames, frames))
    i0 = lax.broadcasted_iota(jnp.int32, (frames, frames), 0)
    i1 = lax.broadcasted_iota(jnp.int32, (frames, frames), 1)
    seg_col = jnp.sum(jnp.where(i0 == i1, seg_row, 0.0), axis=1, keepdims=True)
    bias[...] = jnp.where(seg_col == seg_row, 0.0, -jnp.inf)
    acc[...] = jnp.zeros_like(acc)
    loads[3].wait()

    scale = HEAD ** (-0.5)
    q_gain, k_gain = qgain_ref[...], kgain_ref[...]

    @pl.loop(0, chunks)
    def _(c):
        stay(c).wait()
        for k in range(1, n_dp):
            came = lax.rem(me + n_dp - k, n_dp)
            pltpu.make_async_remote_copy(
                src_ref=send.at[c, came], dst_ref=recv.at[c, came],
                send_sem=send_sem.at[c, k], recv_sem=recv_sem.at[c, k],
                device_id={"dp": came}, device_id_type=MESH,
            ).wait_recv()
        blocks = [recv[c, s].astype(F32) for s in range(n_dp)]
        for i in range(PER):
            cols = pl.ds(pl.multiple_of(c * width + i * HEAD, HEAD), HEAD)

            def packed(a):
                at = (3 * i + a) * padded
                return jnp.concatenate([b[at:at + rows] for b in blocks], axis=0)

            q, k, v = packed(0), packed(1), packed(2).astype(BF16)
            g = g_in[:, cols]
            q_inv = lax.rsqrt(jnp.mean(q * q, axis=-1, keepdims=True) + 1e-06)
            k_inv = lax.rsqrt(jnp.mean(k * k, axis=-1, keepdims=True) + 1e-06)
            q_unit, k_unit = q * q_inv, k * k_inv
            q_norm, k_norm = (q_unit * q_gain).astype(BF16), (k_unit * k_gain).astype(BF16)
            scores = mm(k_norm, q_norm, (1, 1)) + bias[...]
            top = jnp.max(scores, axis=0, keepdims=True)
            e = jnp.exp2((scores - top) * (scale * math.log2(math.e)))
            probs = e * (1.0 / jnp.sum(e, axis=0, keepdims=True))
            half = probs.astype(BF16)
            d_prob = mm(v, g, (1, 1))
            delta = jnp.sum(half.astype(F32) * d_prob, axis=0, keepdims=True)
            d_score = (probs * (d_prob - delta) * scale).astype(BF16)
            vgrad_ref[:, cols] = mm(half, g, (1, 0)).astype(BF16)
            d_k = mm(d_score, q_norm, (1, 0))
            d_q = mm(d_score, k_norm, (0, 0))
            for out, at, d_norm, unit, inv, gain in (
                (qgrad_ref, 0, d_q, q_unit, q_inv, q_gain),
                (kgrad_ref, 1, d_k, k_unit, k_inv, k_gain),
            ):
                both = d_norm * unit
                acc[at] += jnp.sum(both.reshape(frames // 8, 8, HEAD), axis=0)
                inner = jnp.mean(both * gain, axis=-1, keepdims=True)
                out[:, cols] = (inv * (d_norm * gain - unit * inner)).astype(BF16)

    def exchange(axis, n, mine, slots, ssem, rsem):
        copies = []
        for k in range(1, n):
            copy = pltpu.make_async_remote_copy(
                src_ref=slots.at[mine], dst_ref=slots.at[mine],
                send_sem=ssem.at[k], recv_sem=rsem.at[k],
                device_id={axis: lax.rem(mine + k, n)}, device_id_type=MESH,
            )
            copy.start()
            copies.append(copy)
        for k in range(1, n):
            came = lax.rem(mine + n - k, n)
            pltpu.make_async_remote_copy(
                src_ref=slots.at[came], dst_ref=slots.at[came],
                send_sem=ssem.at[k], recv_sem=rsem.at[k],
                device_id={axis: came}, device_id_type=MESH,
            ).wait_recv()
        return copies

    red_dp[me] = jnp.sum(acc[...], axis=1)
    sent = exchange("dp", n_dp, me, red_dp, dp_send, dp_recv)
    total = red_dp[0]
    for s in range(1, n_dp):
        total = total + red_dp[s]
    red_fs[mf] = total
    sent += exchange("fsdp", n_fs, mf, red_fs, fs_send, fs_recv)
    total = red_fs[0]
    for s in range(1, n_fs):
        total = total + red_fs[s]
    qsum_ref[...] = total[0:1]
    ksum_ref[...] = total[1:2]
    for copy in sent:
        copy.wait_send()

    @pl.loop(0, chunks)
    def _(c):
        for k in range(1, n_dp):
            hop(c, k).wait_send()


def on_device(n_dp, n_fs, query_in, key_in, value_in, length_plan, segment_ids, out_grad, query_gain, key_gain):
    frames, hid = query_in.shape
    rows = frames // n_dp
    padded = -(-rows // 8) * 8
    chunks = hid // (PER * HEAD)
    vmem = pl.BlockSpec(memory_space=pltpu.VMEM)
    hbm = pl.BlockSpec(memory_space=pl.ANY)
    wide = jax.ShapeDtypeStruct((frames, hid), BF16)
    line = jax.ShapeDtypeStruct((1, HEAD), F32)
    dma = pltpu.SemaphoreType.DMA
    outs = pl.pallas_call(
        functools.partial(kernel, n_dp, n_fs),
        out_shape=(wide, wide, wide, line, line),
        in_specs=[hbm, hbm, hbm, vmem, vmem, hbm, vmem, vmem],
        out_specs=(vmem,) * 5,
        scratch_shapes=[
            pltpu.VMEM((frames, hid), BF16),
            pltpu.VMEM((frames, hid), BF16),
            pltpu.VMEM((frames, hid), BF16),
            pltpu.VMEM((frames, hid), BF16),
            pltpu.VMEM((chunks, n_dp, 3 * PER * padded, HEAD), BF16),
            pltpu.VMEM((chunks, n_dp, 3 * PER * padded, HEAD), BF16),
            pltpu.VMEM((n_dp * padded, frames), BF16),
            pltpu.VMEM((frames, frames), F32),
            pltpu.VMEM((2, 8, HEAD), F32),
            pltpu.VMEM((n_dp, 2, HEAD), F32),
            pltpu.VMEM((n_fs, 2, HEAD), F32),
            dma((4,)),
            dma((chunks, n_dp)),
            dma((chunks, n_dp)),
            dma((n_dp,)),
            dma((n_dp,)),
            dma((n_fs,)),
            dma((n_fs,)),
        ],
        compiler_params=pltpu.CompilerParams(
            collective_id=0, has_side_effects=True, vmem_limit_bytes=32 * 1024 * 1024
        ),
    )(
        query_in, key_in, value_in, length_plan, segment_ids, out_grad,
        query_gain.reshape(1, HEAD), key_gain.reshape(1, HEAD),
    )
    q_grad, k_grad, v_grad, q_sum, k_sum = outs
    return (q_grad, k_grad, v_grad, q_sum.reshape(HEAD), k_sum.reshape(HEAD))


def solution(mesh):
    split = P(("dp", "fsdp"), None)
    return jax.shard_map(
        functools.partial(on_device, mesh.shape["dp"], mesh.shape["fsdp"]),
        mesh=mesh,
        in_specs=(split,) * 6 + (P(), P()),
        out_specs=(split,) * 3 + (P(), P()),
        check_vma=False,
    )
```

```python
import functools
import math

import jax
import jax.numpy as jnp
from jax import lax
from jax.experimental import pallas as pl
from jax.experimental.pallas import tpu as pltpu
from jax.sharding import PartitionSpec as P

HEAD = 128
PER = 2
AHEAD = 2
GRANT = 60 * 1024 * 1024
MESH = pl.DeviceIdType.MESH
F32, BF16 = jnp.float32, jnp.bfloat16


def mm(a, b, contract):
    return lax.dot_general(a, b, ((contract[:1], contract[1:]), ((), ())), preferred_element_type=F32)


def kernel(
    n_dp, n_fs,
    q_hbm, k_hbm, v_hbm, plan_hbm, seg_hbm, g_hbm, qgain_hbm, kgain_hbm,
    qgrad_hbm, kgrad_hbm, vgrad_hbm, qsum_ref, ksum_ref,
    qgrad_ref, kgrad_ref, vgrad_ref, out_sem,
    q_in, k_in, v_in, g_in, plan_ref, seg_ref, qgain_ref, kgain_ref,
    send, recv, onehot, bias, acc, red_dp, red_fs,
    in_sem, small_sem, send_sem, recv_sem, dp_send, dp_recv, fs_send, fs_recv,
):
    frames = q_in.shape[0]
    rows = frames // n_dp
    chunks, _, height, _ = send.shape
    padded = height // (3 * PER)
    width = PER * HEAD
    me = lax.axis_index("dp")
    mf = lax.axis_index("fsdp")

    def load(i, c):
        src, dst = ((q_hbm, q_in), (k_hbm, k_in), (v_hbm, v_in), (g_hbm, g_in))[i]
        cols = pl.ds(pl.multiple_of(c * width, width), width)
        return pltpu.make_async_copy(src.at[:, cols], dst.at[:, cols], in_sem.at[i, c])

    small = [
        pltpu.make_async_copy(src, dst, small_sem.at[i])
        for i, (src, dst) in enumerate(
            ((plan_hbm, plan_ref), (seg_hbm, seg_ref), (qgain_hbm, qgain_ref), (kgain_hbm, kgain_ref))
        )
    ]
    for copy in small:
        copy.start()
    for c in range(chunks):
        for i in range(3):
            load(i, c).start()
    for c in range(chunks):
        load(3, c).start()
    barrier = pltpu.get_barrier_semaphore()
    for k in range(1, n_dp):
        pl.semaphore_signal(barrier, inc=1, device_id={"dp": lax.rem(me + k, n_dp)}, device_id_type=MESH)
    for k in range(1, n_fs):
        pl.semaphore_signal(barrier, inc=1, device_id={"fsdp": lax.rem(mf + k, n_fs)}, device_id_type=MESH)

    order = lax.broadcasted_iota(jnp.int32, (n_dp * padded, 1), 0)
    if padded != rows:
        within = order % padded
        order = jnp.where(within < rows, order // padded * rows + within, -1)
    small[0].wait()
    onehot[...] = (order == plan_ref[...]).astype(F32).astype(BF16)

    def store(i, c):
        src, dst = ((qgrad_ref, qgrad_hbm), (kgrad_ref, kgrad_hbm), (vgrad_ref, vgrad_hbm))[i]
        cols = pl.ds(pl.multiple_of(c * width, width), width)
        return pltpu.make_async_copy(src.at[:, cols], dst.at[:, cols], out_sem.at[i, c])

    def hop(c, k):
        to = lax.rem(me + k, n_dp)
        return pltpu.make_async_remote_copy(
            src_ref=send.at[c, to], dst_ref=recv.at[c, me],
            send_sem=send_sem.at[c, k], recv_sem=recv_sem.at[c, k],
            device_id={"dp": to}, device_id_type=MESH,
        )

    def stay(c):
        return pltpu.make_async_copy(send.at[c, me], recv.at[c, me], recv_sem.at[c, 0])

    def gather(c):
        for i in range(3):
            load(i, c).wait()
        cols = pl.ds(pl.multiple_of(c * width, width), width)
        sorted_rows = [mm(onehot[...], ref[:, cols], (1, 0)) for ref in (q_in, k_in, v_in)]
        for d in range(n_dp):
            span = slice(d * padded, (d + 1) * padded)
            send[c, d] = jnp.concatenate(
                [x[span, i * HEAD:(i + 1) * HEAD] for i in range(PER) for x in sorted_rows], axis=0
            ).astype(BF16)

    def launch(c):
        for k in range(1, n_dp):
            hop(c, k).start()
        stay(c).start()

    gather(0)
    pl.semaphore_wait(barrier, n_dp - 1 + n_fs - 1)
    launch(0)

    for c in range(1, min(AHEAD, chunks)):
        gather(c)
        launch(c)

    @pl.loop(min(AHEAD, chunks), chunks)
    def _(c):
        gather(c)

    for copy in small[1:]:
        copy.wait()
    seg_row = jnp.broadcast_to(seg_ref[...].astype(F32), (frames, frames))
    i0 = lax.broadcasted_iota(jnp.int32, (frames, frames), 0)
    i1 = lax.broadcasted_iota(jnp.int32, (frames, frames), 1)
    seg_col = jnp.sum(jnp.where(i0 == i1, seg_row, 0.0), axis=1, keepdims=True)
    bias[...] = jnp.where(seg_col == seg_row, 0.0, -jnp.inf)
    acc[...] = jnp.zeros_like(acc)
    for c in range(chunks):
        load(3, c).wait()

    scale = HEAD ** (-0.5)
    q_gain, k_gain = qgain_ref[...], kgain_ref[...]

    @pl.loop(0, chunks)
    def _(c):
        for k in range(1, n_dp):
            hop(c, k).wait_send()

        @pl.when(c + AHEAD < chunks)
        def _():
            launch(c + AHEAD)

        stay(c).wait()
        for k in range(1, n_dp):
            came = lax.rem(me + n_dp - k, n_dp)
            pltpu.make_async_remote_copy(
                src_ref=send.at[c, came], dst_ref=recv.at[c, came],
                send_sem=send_sem.at[c, k], recv_sem=recv_sem.at[c, k],
                device_id={"dp": came}, device_id_type=MESH,
            ).wait_recv()
        blocks = [recv[c, s].astype(F32) for s in range(n_dp)]
        for i in range(PER):
            cols = pl.ds(pl.multiple_of(c * width + i * HEAD, HEAD), HEAD)

            def packed(a):
                at = (3 * i + a) * padded
                return jnp.concatenate([b[at:at + rows] for b in blocks], axis=0)

            q, k, v = packed(0), packed(1), packed(2).astype(BF16)
            g = g_in[:, cols]
            q_inv = lax.rsqrt(jnp.mean(q * q, axis=-1, keepdims=True) + 1e-06)
            k_inv = lax.rsqrt(jnp.mean(k * k, axis=-1, keepdims=True) + 1e-06)
            q_unit, k_unit = q * q_inv, k * k_inv
            q_norm, k_norm = (q_unit * q_gain).astype(BF16), (k_unit * k_gain).astype(BF16)
            scores = mm(k_norm, q_norm, (1, 1)) + bias[...]
            top = jnp.max(scores, axis=0, keepdims=True)
            e = jnp.exp2((scores - top) * (scale * math.log2(math.e)))
            probs = e * (1.0 / jnp.sum(e, axis=0, keepdims=True))
            half = probs.astype(BF16)
            d_prob = mm(v, g, (1, 1))
            delta = jnp.sum(half.astype(F32) * d_prob, axis=0, keepdims=True)
            d_score = (probs * (d_prob - delta) * scale).astype(BF16)
            vgrad_ref[:, cols] = mm(half, g, (1, 0)).astype(BF16)
            d_k = mm(d_score, q_norm, (1, 0))
            d_q = mm(d_score, k_norm, (0, 0))
            for out, at, d_norm, unit, inv, gain in (
                (qgrad_ref, 0, d_q, q_unit, q_inv, q_gain),
                (kgrad_ref, 1, d_k, k_unit, k_inv, k_gain),
            ):
                both = d_norm * unit
                acc[at] += jnp.sum(both.reshape(frames // 8, 8, HEAD), axis=0)
                inner = jnp.mean(both * gain, axis=-1, keepdims=True)
                out[:, cols] = (inv * (d_norm * gain - unit * inner)).astype(BF16)

        for i in range(3):
            store(i, c).start()

    def exchange(axis, n, mine, slots, ssem, rsem):
        copies = []
        for k in range(1, n):
            copy = pltpu.make_async_remote_copy(
                src_ref=slots.at[mine], dst_ref=slots.at[mine],
                send_sem=ssem.at[k], recv_sem=rsem.at[k],
                device_id={axis: lax.rem(mine + k, n)}, device_id_type=MESH,
            )
            copy.start()
            copies.append(copy)
        for k in range(1, n):
            came = lax.rem(mine + n - k, n)
            pltpu.make_async_remote_copy(
                src_ref=slots.at[came], dst_ref=slots.at[came],
                send_sem=ssem.at[k], recv_sem=rsem.at[k],
                device_id={axis: came}, device_id_type=MESH,
            ).wait_recv()
        return copies

    red_dp[me] = jnp.sum(acc[...], axis=1)
    sent = exchange("dp", n_dp, me, red_dp, dp_send, dp_recv)
    total = red_dp[0]
    for s in range(1, n_dp):
        total = total + red_dp[s]
    red_fs[mf] = total
    sent += exchange("fsdp", n_fs, mf, red_fs, fs_send, fs_recv)
    total = red_fs[0]
    for s in range(1, n_fs):
        total = total + red_fs[s]
    qsum_ref[...] = total[0:1]
    ksum_ref[...] = total[1:2]
    for copy in sent:
        copy.wait_send()
    for c in range(chunks):
        for i in range(3):
            store(i, c).wait()


def deliver(*refs):
    count = len(refs) // 2
    sems = refs[-1]
    copies = [pltpu.make_async_copy(refs[i], refs[count + i], sems.at[i]) for i in range(count)]
    for copy in copies:
        copy.start()
    for copy in copies:
        copy.wait()


def on_device(n_dp, n_fs, query_in, key_in, value_in, length_plan, segment_ids, out_grad, query_gain, key_gain):
    frames, hid = query_in.shape
    rows = frames // n_dp
    padded = -(-rows // 8) * 8
    chunks = hid // (PER * HEAD)
    vmem = pl.BlockSpec(memory_space=pltpu.VMEM)
    hbm = pl.BlockSpec(memory_space=pltpu.HBM)
    free = pl.BlockSpec(memory_space=pl.ANY)
    wide = jax.ShapeDtypeStruct((frames, hid), BF16)
    line = jax.ShapeDtypeStruct((1, HEAD), F32)
    dma = pltpu.SemaphoreType.DMA
    outs = pl.pallas_call(
        functools.partial(kernel, n_dp, n_fs),
        out_shape=(wide, wide, wide, line, line),
        in_specs=[hbm] * 8,
        out_specs=(hbm, hbm, hbm, vmem, vmem),
        scratch_shapes=[
            pltpu.VMEM((frames, hid), BF16),
            pltpu.VMEM((frames, hid), BF16),
            pltpu.VMEM((frames, hid), BF16),
            dma((3, chunks)),
            pltpu.VMEM((frames, hid), BF16),
            pltpu.VMEM((frames, hid), BF16),
            pltpu.VMEM((frames, hid), BF16),
            pltpu.VMEM((frames, hid), BF16),
            pltpu.VMEM((1, frames), jnp.int32),
            pltpu.VMEM((1, frames), jnp.int32),
            pltpu.VMEM((1, HEAD), F32),
            pltpu.VMEM((1, HEAD), F32),
            pltpu.VMEM((chunks, n_dp, 3 * PER * padded, HEAD), BF16),
            pltpu.VMEM((chunks, n_dp, 3 * PER * padded, HEAD), BF16),
            pltpu.VMEM((n_dp * padded, frames), BF16),
            pltpu.VMEM((frames, frames), F32),
            pltpu.VMEM((2, 8, HEAD), F32),
            pltpu.VMEM((n_dp, 2, HEAD), F32),
            pltpu.VMEM((n_fs, 2, HEAD), F32),
            dma((4, chunks)),
            dma((4,)),
            dma((chunks, n_dp)),
            dma((chunks, n_dp)),
            dma((n_dp,)),
            dma((n_dp,)),
            dma((n_fs,)),
            dma((n_fs,)),
        ],
        compiler_params=pltpu.CompilerParams(
            collective_id=0, has_side_effects=True, vmem_limit_bytes=GRANT
        ),
    )(
        query_in, key_in, value_in, length_plan, segment_ids, out_grad,
        query_gain.reshape(1, HEAD), key_gain.reshape(1, HEAD),
    )
    q_grad, k_grad, v_grad, q_sum, k_sum = pl.pallas_call(
        deliver,
        out_shape=(wide, wide, wide, line, line),
        in_specs=[free] * 5,
        out_specs=(hbm,) * 5,
        scratch_shapes=[dma((5,))],
        compiler_params=pltpu.CompilerParams(vmem_limit_bytes=GRANT),
    )(*outs)
    return (q_grad, k_grad, v_grad, q_sum.reshape(HEAD), k_sum.reshape(HEAD))


def solution(mesh):
    split = P(("dp", "fsdp"), None)
    return jax.shard_map(
        functools.partial(on_device, mesh.shape["dp"], mesh.shape["fsdp"]),
        mesh=mesh,
        in_specs=(split,) * 6 + (P(), P()),
        out_specs=(split,) * 3 + (P(), P()),
        check_vma=False,
    )
```
